32 devices in a mesh: sub: 8 (over z, x), grp: 4 (over y, core).
Axes of the slice: x: 2, y: 2, z: 4, core: 2. Of those that a mesh axis runs over, the one named last changes fastest.
Arguments:
- gap: bfloat16 [256, 256, 128], P(('sub', 'grp')), may hold values from -120 to 120
- inverse_blocks: bfloat16 [256, 256, 256], P(('sub', 'grp')), may hold values from -1 to 7, as said below
- corner_maps: bfloat16 [256, 24, 256], P(('sub', 'grp')), may hold values from -0.375 to 0.375
- coarse_inverse: float32 [8, 256, 256], P('sub'), may hold values from -1 to 7, as said below
- partner_slots: int32 [256, 2], P(('sub', 'grp')), may hold values from 0 to 7, as said below
- face_sizes: int32 [256, 2], P(('sub', 'grp')), may hold values from 32 to 128, as said below
- owners: int32 [256, 4], P(('sub', 'grp')), may hold values from 0 to 7, all different within a row; in each aligned block of 8 rows (0 to 7, 8 to 15, ...) at most 8 rows name the same one
- corner_lists: int32 [256, 24], P(('sub', 'grp')), may hold values from 0 to 255
Outputs:
- solution: float32 [256, 256, 128], P(('sub', 'grp'))
The draws below stay inside these ranges and needn't reach their ends.
Inputs may be any that keep to these rules, and one draw needn't show every extreme that they name: `partner_slots`: the pairing is mutual: if face 0 of s names t, face 0 of t names s, and likewise for face 1. `face_sizes`: partners across a face have equal sizes. `owners`: each subdomain names 4 different tiles; among the 8 subdomains of one device no tile is named more than 8 times. `inverse_blocks`: each block is symmetric positive definite. `coarse_inverse`: each tile is symmetric positive definite.
All inputs are finite; a program needn't handle non-finite values.
Results may differ from the reference program's by a relative error of at most 0.00083.
Values sent between devices are 32-bit elements; how exact they have to be, the bound alone decides.
A program may use at most 64 MiB of HBM per device.

```python
import math
import jax
import jax.numpy as jnp
import numpy as np
from jax import lax

SLOTS = 8
H = 128
B = 256
R = 128
NCS = 24
GROUPS = 4
K = 256
ITERS = 2
CAP = 8
SUBD = 256
N_SUB = 8
N_GRP = 4


def pairing(key):
    devices = N_SUB * N_GRP
    device = jnp.arange(devices, dtype=jnp.int32)
    sub_index = device // N_GRP
    grp_index = device % N_GRP
    slot_list = []
    size_list = []
    for face, flip in ((0, 1), (1, N_SUB // 2)):
        perm_key = jax.random.fold_in(key, 11 + face)
        length_key = jax.random.fold_in(key, 21 + face)
        perms = jax.vmap(lambda single: jax.random.permutation(single, SLOTS))(jax.random.split(perm_key, devices)).astype(jnp.int32)
        inverse = jnp.argsort(perms, axis=1, stable=True).astype(jnp.int32)
        partner = jnp.bitwise_xor(sub_index, flip) * N_GRP + grp_index
        lower = (sub_index // flip % 2 == 0)[:, None]
        slots_face = jnp.where(lower, perms, inverse[partner])
        lengths = jax.random.randint(length_key, (devices, SLOTS), H // 4, H + 1).astype(jnp.int32)
        lengths = lengths.at[:, 0].set(H)
        upper_lengths = jnp.take_along_axis(lengths[partner], inverse[partner], axis=1)
        sizes_face = jnp.where(lower, lengths, upper_lengths)
        slot_list.append(slots_face.reshape(-1))
        size_list.append(sizes_face.reshape(-1))
    return (jnp.stack(slot_list, axis=1), jnp.stack(size_list, axis=1))


def draw_partner_slots(key, part):
    return pairing(key)[0]


def draw_face_sizes(key, part):
    return pairing(key)[1]


def dominant(key, count, order):
    keys = jax.random.split(key, 2)
    spread = jax.random.uniform(keys[0], (count, order, order), minval=-1.0, maxval=1.0) * (2.0 / order)
    offdiag = 0.5 * (spread + jnp.swapaxes(spread, 1, 2))
    identity = jnp.eye(order, dtype=jnp.float32)[None]
    diagonal = jax.random.uniform(keys[1], (count, order, 1), minval=2.2, maxval=3.5)
    return offdiag * (1.0 - identity) + identity * diagonal


def draw_inverse_blocks(key, part):
    return dominant(jax.random.fold_in(key, 31), SUBD, B).astype(jnp.bfloat16)


def draw_coarse_inverse(key, part):
    return dominant(jax.random.fold_in(key, 41), N_SUB, K).astype(jnp.float32)


def draw_gap(key, part):
    keys = jax.random.split(jax.random.fold_in(key, 51), 3)
    devices = N_SUB * N_GRP
    rise = 3.0 ** ((jnp.arange(SUBD) // SLOTS).astype(jnp.float32) / max(devices - 1, 1))
    row_scale = jnp.exp(jax.random.uniform(keys[1], (SUBD, B, 1), minval=0.0, maxval=math.log(10.0)))
    column_scale = jnp.exp(jax.random.uniform(keys[2], (1, 1, R), minval=0.0, maxval=math.log(10.0)))
    base = jnp.clip(jax.random.normal(keys[0], (SUBD, B, R)), -4.0, 4.0)
    return (0.1 * base * rise[:, None, None] * row_scale * column_scale).astype(jnp.bfloat16)


def place_ends(drawn, key, least, largest):
    index_at = [jax.random.randint(jax.random.fold_in(key, axis), (), 0, length) for axis, length in enumerate(drawn.shape)]
    widest = drawn.shape.index(max(drawn.shape))
    next_to = index_at[:widest] + [(index_at[widest] + 1) % drawn.shape[widest]] + index_at[widest + 1:]
    return drawn.at[tuple(index_at)].set(least).at[tuple(next_to)].set(largest)


def block_levels(own_key, shape, pieces, least, largest):
    factor_of, own = 1.0, jax.random.fold_in(own_key, 6)
    for position, blocks in pieces:
        heights = jnp.exp(jax.random.uniform(jax.random.fold_in(own, position), (blocks,), jnp.float32, least / len(pieces), largest / len(pieces)))
        factor_of = factor_of * jnp.repeat(heights, shape[position] // blocks).reshape([-1 if axis == position else 1 for axis in range(len(shape))])
    return factor_of


def assign_block(key, own, number, rows, count, top, reach, lean):
    ranking = jax.random.permutation(key, count)
    heavy_load, common = portions_of(count, rows * top, reach, lean, True), portions_of(count, rows * top, reach, lean, False)
    places = jnp.arange(count)

    def named(tallies, turn):
        used = int((tallies > 0).sum())
        fixed = max(1, used // 4)
        passed = fixed + (places - fixed + turn * (used - fixed)) % max(1, count - fixed)
        return jnp.zeros((count,), jnp.int32).at[ranking[jnp.where(places < fixed, places, passed)]].set(jnp.asarray(tallies, jnp.int32))

    tallies = jnp.where(number % 4 == 0, named(heavy_load, number // 4), named(common, number - number // 4 - 1))
    mixed = jax.random.permutation(jax.random.fold_in(own, 3), count)
    source_of, sink = mixed[0:count // 2 * 2:2], mixed[1:count // 2 * 2:2]
    margin = jnp.minimum(tallies[source_of] - 1, reach - tallies[sink]) // 2
    margin = jnp.where((source_of == ranking[0]) | (sink == ranking[0]) | (tallies[sink] == 0), 0, jnp.maximum(margin, 0))
    passed = jax.random.randint(jax.random.fold_in(own, 4), (count // 2,), 0, 1 << 20) % (margin + 1)
    tallies = tallies.at[source_of].add(-passed).at[sink].add(passed)
    items = jnp.searchsorted(jnp.cumsum(tallies), jnp.arange(rows * top), side="right").astype(jnp.int32)
    grid = items.reshape(top, rows).T
    grid = grid[jax.random.permutation(jax.random.fold_in(own, 1), rows)]
    turn = jax.random.randint(jax.random.fold_in(own, 2), (rows, 1), 0, top)
    return jnp.take_along_axis(grid, (jnp.arange(top)[None, :] + turn) % top, axis=1)


def portions_of(number_of, total, most, lean, full):
    loads = [(1 << 20) // math.isqrt(grade ** lean) + 1 for grade in range(1, number_of + 1)]
    largest = most if full else min(most, max(-(-total // number_of), total * loads[0] // sum(loads)))
    least = 1 if total - largest >= number_of - 1 else 0
    counts, rest = [largest] + [least] * (number_of - 1), total - largest - least * (number_of - 1)
    while rest > 0:
        free = [i for i in range(1, number_of) if counts[i] < largest] or [i for i in range(1, number_of) if counts[i] < most]
        pool, budget = sum([loads[i] for i in free]), rest
        for i in free:
            more = min(most - counts[i], max(1, budget * loads[i] // pool), rest)
            counts[i] = counts[i] + more
            rest = rest - more
    return np.array(counts)


def noise(stream_key, shape, deviation, most, cuts=(), held_as=jnp.bfloat16):
    loudness = block_levels(stream_key, shape, cuts, -0.22, 0.18) if cuts else 1.0
    result = jax.random.normal(stream_key, shape, jnp.float32) * deviation * loudness
    return jnp.minimum(jnp.maximum(result, -most), most).astype(held_as)


def setup_inputs(seed: int = 0) -> dict:
    seeds = jax.random.split(jax.random.key(seed), 9)
    gap = draw_gap(jax.random.fold_in(seeds[8], 71), 0)
    inverse_blocks = draw_inverse_blocks(jax.random.fold_in(seeds[8], 71), 0)
    corner_maps = noise(seeds[2], (SUBD, NCS, B), B ** -0.5, 0.375, ((0, 32),))
    coarse_inverse = draw_coarse_inverse(jax.random.fold_in(seeds[8], 71), 0)
    partner_slots = draw_partner_slots(jax.random.fold_in(seeds[8], 71), 0)
    face_sizes = draw_face_sizes(jax.random.fold_in(seeds[8], 71), 0)
    owners_keys = jax.random.split(jax.random.fold_in(seeds[6], 1), SUBD // SLOTS)
    owners_turns = jax.random.permutation(jax.random.fold_in(seeds[6], 3), SUBD // SLOTS)
    owners = jax.vmap(lambda own, number: assign_block(jax.random.fold_in(seeds[6], 2), own, number, SLOTS, N_SUB, GROUPS, CAP, 2))(owners_keys, owners_turns).reshape((SUBD, GROUPS))
    corner_lists = place_ends(jax.random.randint(seeds[7], (SUBD, NCS), 0, K), jax.random.fold_in(seeds[7], 1), 0, K - 1).astype(jnp.int32)
    return dict(gap=gap, inverse_blocks=inverse_blocks, corner_maps=corner_maps, coarse_inverse=coarse_inverse, partner_slots=partner_slots, face_sizes=face_sizes, owners=owners, corner_lists=corner_lists)


def reference(gap, inverse_blocks, corner_maps, coarse_inverse, partner_slots, face_sizes, owners, corner_lists):
    highest = lax.Precision.HIGHEST
    count = gap.shape[0]
    devices = count // SLOTS
    index = jnp.arange(count, dtype=jnp.int32)
    device = index // SLOTS
    sub_index = device // N_GRP
    grp_index = device % N_GRP
    near_part = (jnp.bitwise_xor(sub_index, 1) * N_GRP + grp_index) * SLOTS + partner_slots[:, 0]
    far_part = (jnp.bitwise_xor(sub_index, N_SUB // 2) * N_GRP + grp_index) * SLOTS + partner_slots[:, 1]
    rows = jnp.arange(2 * H, dtype=jnp.int32)
    upper = rows >= H
    within = rows - H * upper.astype(jnp.int32)
    limit = jnp.where(upper[None, :], face_sizes[:, 1:2], face_sizes[:, 0:1])
    mask = (within[None, :] < limit).astype(jnp.float32)[:, :, None]

    def jump(field):
        near = field[:, :H] - field[near_part, :H]
        far = field[:, H:] - field[far_part, H:]
        return jnp.concatenate([near, far], axis=1) * mask

    owner_each = jnp.repeat(owners, NCS // GROUPS, axis=1)
    corner_rows = (owner_each * K + corner_lists).astype(jnp.int32)
    flat_rows = corner_rows.reshape(-1)
    maps_wide = corner_maps.astype(jnp.float32)

    def local_solve(blocks):
        inverse, maps, jumps = blocks
        jumps = jumps.astype(jnp.float32)
        solved = jnp.einsum('sij,sjr->sir', inverse.astype(jnp.float32), jumps, precision=highest)
        corners = jnp.einsum('scj,sjr->scr', maps.astype(jnp.float32), jumps, precision=highest)
        return solved, corners

    def apply(field):
        jumped = jump(field).astype(jnp.bfloat16)
        grouped = (inverse_blocks.reshape(devices, SLOTS, 2 * H, 2 * H),
                   corner_maps.reshape(devices, SLOTS, NCS, 2 * H),
                   jumped.reshape(devices, SLOTS, 2 * H, R))
        solved, corners = lax.map(local_solve, grouped)
        solved = solved.reshape(count, 2 * H, R)
        corners = corners.reshape(count * NCS, R)
        tiles = jnp.zeros((N_SUB * K, R), jnp.float32).at[flat_rows].add(corners).reshape(N_SUB, K, R)
        coarse = jnp.einsum('okj,ojr->okr', coarse_inverse, tiles, precision=highest).reshape(N_SUB * K, R)
        picked = coarse[corner_rows]
        lifted = solved + jnp.einsum('scj,scr->sjr', maps_wide, picked, precision=highest)
        return jump(lifted)

    residual = jump(gap.astype(jnp.float32))
    direction = residual
    solution = jnp.zeros_like(residual)
    norm_now = jnp.sum(residual * residual, axis=(0, 1))
    for iteration in range(ITERS):
        image = apply(direction)
        alpha = norm_now / jnp.sum(direction * image, axis=(0, 1))
        solution = solution + alpha * direction
        if iteration + 1 < ITERS:
            residual = residual - alpha * image
            norm_next = jnp.sum(residual * residual, axis=(0, 1))
            direction = residual + (norm_next / norm_now) * direction
            norm_now = norm_next
    return solution
```

```python
import functools

import jax
import jax.numpy as jnp
from jax import lax
from jax.experimental import pallas as pl
from jax.experimental.pallas import tpu as pltpu
from jax.sharding import PartitionSpec as P

MESH = pl.DeviceIdType.MESH
HIGHEST = lax.Precision.HIGHEST
F32 = jnp.float32
NN = (((1,), (0,)), ((), ()))
NT = (((1,), (1,)), ((), ()))
TN = (((0,), (0,)), ((), ()))


def dot(a, b, dims=NN, precision=None):
    return lax.dot_general(a, b, dims, precision=precision, preferred_element_type=F32)


def each(low, high, step):
    if high - low <= 16:
        for i in range(low, high):
            step(i)
    else:
        lax.fori_loop(low, high, lambda i, c: (step(i), c)[1], 0)


def fold(x):
    rows, columns = x.shape
    return jnp.sum(x.reshape(rows // 8, 8, columns), axis=0)


def kernel(
    n_sub, n_grp, dims,
    gap, inverse, cmap, coarse, pslots, fsizes, owners, owners_v, lists,
    out,
    mine, field, theirs, resid, fbuf, ybuf, image,
    spread, spread_t, idx_out, idx_in, pick, cbuf, cin, tile, tile_in, zfull, qbuf, rbuf, rin,
    arbuf, ar_grp, ar_sub,
    x_send, x_recv, i_send, i_recv, c_send, c_recv, t_send, t_recv, z_send, z_recv, r_send, r_recv,
    g_send, g_recv, s_send, s_recv,
):
    slots, half, columns, per, groups, tile_rows = dims
    ncs = per * groups
    sub = lax.axis_index("sub")
    grp = lax.axis_index("grp")
    top = n_sub // 2

    def flip(bit):
        return sub + bit - 2 * bit * (sub // bit % 2)

    def sub_peer(d):
        return lax.rem(sub + d, n_sub)

    def sub_source(d):
        return lax.rem(sub + n_sub - d, n_sub)

    def grp_peer(d):
        return lax.rem(grp + d, n_grp)

    def grp_source(d):
        return lax.rem(grp + n_grp - d, n_grp)

    def remote(src, dst, send, recv, to_sub, to_grp):
        return pltpu.make_async_remote_copy(
            src_ref=src, dst_ref=dst, send_sem=send, recv_sem=recv,
            device_id=(to_sub, to_grp), device_id_type=MESH,
        )

    barrier = pltpu.get_barrier_semaphore()
    each(1, n_sub, lambda d: pl.semaphore_signal(
        barrier, inc=1, device_id=(sub_peer(d), grp), device_id_type=MESH))
    each(1, n_grp, lambda d: pl.semaphore_signal(
        barrier, inc=1, device_id=(sub, grp_peer(d)), device_id_type=MESH))

    for s in range(slots):
        wide = gap[s].astype(F32)
        mine[0, s] = wide[:half]
        mine[1, s] = wide[half:]
    pl.semaphore_wait(barrier, n_sub + n_grp - 2)

    def swap(turn, face, s, source):
        return remote(
            source.at[face, s], theirs.at[turn, face, s], x_send.at[turn, face, s],
            x_recv.at[turn, face, s], flip(top) if face else flip(1), grp)

    for face in (1, 0):
        for s in range(slots):
            swap(0, face, s, mine).start()

    def index_swap(d, peer_out, slot_in):
        return remote(idx_out.at[peer_out], idx_in.at[slot_in], i_send.at[d], i_recv.at[d],
                      sub_peer(d), grp)

    lane = lax.broadcasted_iota(jnp.int32, (slots, ncs), 1)
    lane_group = jnp.zeros_like(lane)
    for t in range(1, groups):
        lane_group = lane_group + (lane >= per * t).astype(jnp.int32)
    owner_lane = jnp.zeros_like(lane)
    for g in range(groups):
        owner_lane = jnp.where(lane_group == g, owners_v[:, g:g + 1], owner_lane)
    idx_out[...] = jnp.full(idx_out.shape, -1, jnp.int32)

    def index_for(o):
        idx_out[o, :, 0:ncs] = jnp.where(owner_lane == o, lists[...], -1)

    each(0, n_sub, index_for)
    each(1, n_sub, lambda d: index_swap(d, sub_peer(d), sub).start())
    idx_in[sub] = idx_out[sub]

    shape = (n_sub * per, ncs)
    row = lax.broadcasted_iota(jnp.int32, shape, 0)
    col = lax.broadcasted_iota(jnp.int32, shape, 1)
    col_group = jnp.zeros_like(col)
    for t in range(1, groups):
        col_group = col_group + (col >= per * t).astype(jnp.int32)
    row_tile = jnp.zeros_like(row)
    if n_sub <= 16:
        for t in range(1, n_sub):
            row_tile = row_tile + (row >= per * t).astype(jnp.int32)
    else:
        row_tile = lax.fori_loop(
            1, n_sub, lambda t, a: a + (row >= per * t).astype(jnp.int32), row_tile)
    same = (row - per * row_tile) == (col - per * col_group)
    for s in range(slots):
        named = jnp.full(shape, owners[s, 0], jnp.int32)
        for g in range(1, groups):
            named = jnp.where(col_group == g, owners[s, g], named)
        select = jnp.where(same & (named == row_tile), 1.0, 0.0).astype(jnp.bfloat16)
        ordered = dot(select, cmap[s])
        spread[s] = ordered.astype(jnp.bfloat16)
        spread_t[s] = ordered.T

    each(1, n_sub, lambda d: index_swap(d, sub_peer(d), sub_source(d)).wait())
    index = idx_in[...].reshape(n_sub * slots, idx_in.shape[-1])
    place = lax.broadcasted_iota(jnp.int32, (n_sub * slots, tile_rows), 1)
    for j in range(per):
        hit = jnp.zeros((n_sub * slots, tile_rows), F32)
        for g in range(groups):
            c = per * g + j
            hit = hit + jnp.where(index[:, c:c + 1] == place, 1.0, 0.0)
        pick[:, j] = hit.reshape(n_sub, slots, tile_rows)

    arbuf[...] = jnp.zeros_like(arbuf)
    qbuf[...] = jnp.zeros_like(qbuf)
    row_in = lax.broadcasted_iota(jnp.int32, (half, columns), 0)

    def jump(turn, face, s, source):
        other = theirs[turn, face, pslots[s, face]]
        return jnp.where(row_in < fsizes[s, face], source[face, s] - other, 0.0)

    def corners_out(turn, s):
        cbuf[turn, :, s, :] = dot(spread[s], fbuf[s])

    def c_copy(turn, d, slot_in):
        return remote(cbuf.at[turn, pl.ds(sub_peer(d) * per, per)], cin.at[turn, slot_in],
                      c_send.at[turn, d], c_recv.at[turn, d], sub_peer(d), grp)

    def t_copy(turn, d, slot_in):
        return remote(tile.at[turn, grp_peer(d)], tile_in.at[turn, slot_in],
                      t_send.at[turn, d], t_recv.at[turn, d], sub, grp_peer(d))

    def coarse_solve(turn):
        each(1, n_sub, lambda d: c_copy(turn, d, sub).start())
        cin[turn, sub] = cbuf[turn, pl.ds(sub * per, per)]
        each(1, n_sub, lambda d: c_copy(turn, d, sub_source(d)).wait())
        terms = cin[turn].reshape(n_sub * per * slots, columns)
        hits = pick[...].reshape(n_sub * per * slots, tile_rows)
        part = dot(terms, hits, TN, HIGHEST)
        tile[turn] = part.reshape(n_grp, columns // n_grp, tile_rows)
        each(1, n_grp, lambda d: t_copy(turn, d, grp).start())
        tile_in[turn, grp] = tile[turn, grp]
        each(1, n_grp, lambda d: t_copy(turn, d, grp_source(d)).wait())
        total = jnp.sum(tile_in[turn], axis=0)
        return total, dot(total, coarse[0], NT, HIGHEST)

    def all_sum(turn):
        def g_copy(d, slot_in):
            return remote(arbuf.at[turn], ar_grp.at[turn, slot_in],
                          g_send.at[turn, d], g_recv.at[turn, d], sub, grp_peer(d))

        def s_copy(d, slot_in):
            return remote(arbuf.at[turn + 2], ar_sub.at[turn, slot_in],
                          s_send.at[turn, d], s_recv.at[turn, d], sub_peer(d), grp)

        each(1, n_grp, lambda d: g_copy(d, grp).start())
        ar_grp[turn, grp] = arbuf[turn]
        each(1, n_grp, lambda d: g_copy(d, grp_source(d)).wait())
        arbuf[turn + 2] = jnp.sum(ar_grp[turn], axis=0)
        each(1, n_sub, lambda d: s_copy(d, sub).start())
        ar_sub[turn, sub] = arbuf[turn + 2]
        each(1, n_sub, lambda d: s_copy(d, sub_source(d)).wait())
        return jnp.sum(ar_sub[turn], axis=0)

    def wait_swap(turn, source):
        for face in (0, 1):
            for s in range(slots):
                swap(turn, face, s, source).wait()

    wait_swap(0, mine)
    squares = jnp.zeros((8, columns), F32)
    for s in range(slots):
        for face in (0, 1):
            value = jump(0, face, s, mine)
            resid[face, s] = value
            fbuf[s, face * half:(face + 1) * half] = (value + value).astype(jnp.bfloat16)
            squares = squares + fold(value * value)
        corners_out(0, s)
    for s in range(slots):
        ybuf[s] = dot(inverse[s], fbuf[s])
    total, solved = coarse_solve(0)

    def z_copy(d, slot_in):
        return remote(zfull.at[grp], zfull.at[slot_in], z_send.at[d], z_recv.at[d], sub, grp_peer(d))

    zfull[grp] = solved
    each(1, n_grp, lambda d: z_copy(d, grp).start())
    each(1, n_grp, lambda d: z_copy(d, grp_source(d)).wait())
    hits = pick[...].reshape(n_sub * per * slots, tile_rows)
    back = dot(hits, zfull[...].reshape(columns, tile_rows), NT, HIGHEST)
    rbuf[...] = back.reshape(n_sub, per, slots, columns)

    def r_copy(d, slot_in):
        return remote(rbuf.at[sub_peer(d)], rin.at[pl.ds(slot_in * per, per)],
                      r_send.at[d], r_recv.at[d], sub_peer(d), grp)

    each(1, n_sub, lambda d: r_copy(d, sub).start())
    rin[pl.ds(sub * per, per)] = rbuf[sub]
    each(1, n_sub, lambda d: r_copy(d, sub_source(d)).wait())

    products = jnp.zeros((8, columns), F32)
    for s in range(slots):
        lifted = ybuf[s] + dot(spread_t[s], rin[:, s, :], NN, HIGHEST)
        field[1, s] = lifted[half:]
        swap(1, 1, s, field).start()
        field[0, s] = lifted[:half]
        swap(1, 0, s, field).start()
        products = products + fold(lifted[:half] * resid[0, s]) + fold(lifted[half:] * resid[1, s])
    arbuf[0, 0:1] = jnp.sum(squares, axis=0, keepdims=True)
    arbuf[0, 1:2] = 2.0 * jnp.sum(products, axis=0, keepdims=True)
    sums = all_sum(0)
    first = sums[0:1]
    energy = sums[1:2]
    alpha = first / energy

    wait_swap(1, field)
    squares = jnp.zeros((8, columns), F32)
    cross = jnp.zeros((8, columns), F32)
    for s in range(slots):
        for face in (0, 1):
            value = jump(1, face, s, field)
            later = resid[face, s] - alpha * value
            image[face, s] = later
            fbuf[s, face * half:(face + 1) * half] = (later + later).astype(jnp.bfloat16)
            squares = squares + fold(later * later)
            cross = cross + fold(later * value)
        corners_out(1, s)
    products = jnp.zeros((8, columns), F32)
    for s in range(slots):
        local = dot(inverse[s], fbuf[s])
        products = products + fold(local[:half] * image[0, s]) + fold(local[half:] * image[1, s])
    total, solved = coarse_solve(1)
    qbuf[grp] = total * solved
    ones = jnp.ones((8, tile_rows), F32)
    coarse_row = dot(ones, qbuf[...].reshape(columns, tile_rows), NT, HIGHEST)[0:1]
    arbuf[1, 0:1] = jnp.sum(squares, axis=0, keepdims=True)
    arbuf[1, 1:2] = jnp.sum(cross, axis=0, keepdims=True)
    arbuf[1, 2:3] = 2.0 * jnp.sum(products, axis=0, keepdims=True) + coarse_row
    sums = all_sum(1)
    new = sums[0:1]
    beta = new / first
    alpha_later = new / (sums[2:3] + 2.0 * beta * sums[1:2] + beta * beta * energy)
    weight = alpha + alpha_later * beta
    for s in range(slots):
        out[s, 0:half] = weight * resid[0, s] + alpha_later * image[0, s]
        out[s, half:2 * half] = weight * resid[1, s] + alpha_later * image[1, s]


def body(n_sub, n_grp, gap, inverse, cmap, coarse, pslots, fsizes, owners, lists):
    slots, width, columns = gap.shape
    half = width // 2
    ncs = cmap.shape[1]
    groups = owners.shape[1]
    per = ncs // groups
    tile_rows = coarse.shape[1]
    part = columns // n_grp
    vmem = pl.BlockSpec(memory_space=pltpu.VMEM)
    smem = pl.BlockSpec(memory_space=pltpu.SMEM)
    faces = pltpu.VMEM((2, slots, half, columns), F32)
    dma = pltpu.SemaphoreType.DMA
    scratch = [
        faces, faces, pltpu.VMEM((2, 2, slots, half, columns), F32), faces,
        pltpu.VMEM((slots, width, columns), jnp.bfloat16),
        pltpu.VMEM((slots, width, columns), F32), faces,
        pltpu.VMEM((slots, n_sub * per, width), jnp.bfloat16),
        pltpu.VMEM((slots, width, n_sub * per), F32),
        pltpu.VMEM((n_sub, slots, 128), jnp.int32),
        pltpu.VMEM((n_sub, slots, 128), jnp.int32),
        pltpu.VMEM((n_sub, per, slots, tile_rows), F32),
        pltpu.VMEM((2, n_sub * per, slots, columns), F32),
        pltpu.VMEM((2, n_sub, per, slots, columns), F32),
        pltpu.VMEM((2, n_grp, part, tile_rows), F32),
        pltpu.VMEM((2, n_grp, part, tile_rows), F32),
        pltpu.VMEM((n_grp, part, tile_rows), F32),
        pltpu.VMEM((n_grp, part, tile_rows), F32),
        pltpu.VMEM((n_sub, per, slots, columns), F32),
        pltpu.VMEM((n_sub * per, slots, columns), F32),
        pltpu.VMEM((4, 8, columns), F32),
        pltpu.VMEM((2, n_grp, 8, columns), F32),
        pltpu.VMEM((2, n_sub, 8, columns), F32),
        dma((2, 2, slots)), dma((2, 2, slots)),
        dma((n_sub,)), dma((n_sub,)),
        dma((2, n_sub)), dma((2, n_sub)),
        dma((2, n_grp)), dma((2, n_grp)),
        dma((n_grp,)), dma((n_grp,)),
        dma((n_sub,)), dma((n_sub,)),
        dma((2, n_grp)), dma((2, n_grp)),
        dma((2, n_sub)), dma((2, n_sub)),
    ]
    return pl.pallas_call(
        functools.partial(kernel, n_sub, n_grp, (slots, half, columns, per, groups, tile_rows)),
        out_shape=jax.ShapeDtypeStruct((slots, width, columns), F32),
        in_specs=[vmem, vmem, vmem, vmem, smem, smem, smem, vmem, vmem],
        out_specs=vmem,
        scratch_shapes=scratch,
        compiler_params=pltpu.CompilerParams(
            collective_id=0, has_side_effects=True, vmem_limit_bytes=56 * 1024 * 1024),
    )(gap, inverse, cmap, coarse, pslots, fsizes, owners, owners, lists)


def solution(mesh):
    wide = P(("sub", "grp"), None, None)
    flat = P(("sub", "grp"), None)
    placed = (wide, wide, wide, P("sub", None, None), flat, flat, flat, flat)
    return jax.shard_map(
        functools.partial(body, mesh.shape["sub"], mesh.shape["grp"]),
        mesh=mesh, in_specs=placed, out_specs=wide, check_vma=False,
    )
```

```python
import functools

import jax
import jax.numpy as jnp
from jax import lax
from jax.experimental import pallas as pl
from jax.experimental.pallas import tpu as pltpu
from jax.sharding import PartitionSpec as P

MESH = pl.DeviceIdType.MESH
VMEM_BYTES = 56 * 1024 * 1024
HIGHEST = lax.Precision.HIGHEST
F32 = jnp.float32
NN = (((1,), (0,)), ((), ()))
NT = (((1,), (1,)), ((), ()))
TN = (((0,), (0,)), ((), ()))


def dot(a, b, dims=NN, precision=None):
    return lax.dot_general(a, b, dims, precision=precision, preferred_element_type=F32)


def each(low, high, step):
    if high - low <= 16:
        for i in range(low, high):
            step(i)
    else:
        lax.fori_loop(low, high, lambda i, c: (step(i), c)[1], 0)


def fold(x):
    rows, columns = x.shape
    return jnp.sum(x.reshape(rows // 8, 8, columns), axis=0)


def kernel(
    n_sub, n_grp, dims,
    gap_in, inverse_in, cmap_in, coarse_in, pslots_in, fsizes_in, owners_in, lists_in,
    resid_out, later_out, weight_out, alpha_out,
    gap, inverse, cmap, coarse, pslots, fsizes, owners, lists, l_sem, o_sem,
    mine, field, near_first, far_first, near_later, far_later, resid, fbuf, ybuf, image,
    spread, spread_t, idx_out, idx_in, pick, cbuf, cin, tile, tile_in, zfull, qbuf, rbuf, rin,
    arbuf, ar_grp, ar_sub,
    x_send, x_recv, i_send, i_recv, c_send, c_recv, t_send, t_recv, z_send, z_recv, r_send, r_recv,
    g_send, g_recv, s_send, s_recv,
):
    slots, half, columns, per, groups, tile_rows = dims
    ncs = per * groups
    sub = lax.axis_index("sub")
    grp = lax.axis_index("grp")
    top = n_sub // 2
    theirs = ((near_first, far_first), (near_later, far_later))

    def flip(bit):
        return sub + bit - 2 * bit * (sub // bit % 2)

    def sub_peer(d):
        return lax.rem(sub + d, n_sub)

    def sub_source(d):
        return lax.rem(sub + n_sub - d, n_sub)

    def grp_peer(d):
        return lax.rem(grp + d, n_grp)

    def grp_source(d):
        return lax.rem(grp + n_grp - d, n_grp)

    def remote(src, dst, send, recv, to_sub, to_grp):
        return pltpu.make_async_remote_copy(
            src_ref=src, dst_ref=dst, send_sem=send, recv_sem=recv,
            device_id=(to_sub, to_grp), device_id_type=MESH,
        )

    loads = [
        pltpu.make_async_copy(source, target, l_sem.at[i])
        for i, (source, target) in enumerate((
            (gap_in, gap), (lists_in, lists), (owners_in, owners), (cmap_in, cmap),
            (inverse_in, inverse), (coarse_in, coarse), (pslots_in, pslots), (fsizes_in, fsizes)))
    ]
    for load in loads:
        load.start()
    barrier = pltpu.get_barrier_semaphore()
    each(1, n_sub, lambda d: pl.semaphore_signal(
        barrier, inc=1, device_id=(sub_peer(d), grp), device_id_type=MESH))
    each(1, n_grp, lambda d: pl.semaphore_signal(
        barrier, inc=1, device_id=(sub, grp_peer(d)), device_id_type=MESH))

    loads[0].wait()
    for s in range(slots):
        wide = gap[s].astype(F32)
        mine[0, s] = wide[:half]
        mine[1, s] = wide[half:]
    pl.semaphore_wait(barrier, n_sub + n_grp - 2)

    def swap(turn, face, s, source):
        return remote(
            source.at[face, s], theirs[turn][face].at[s], x_send.at[turn, face, s],
            x_recv.at[turn, face, s], flip(top) if face else flip(1), grp)

    for face in (1, 0):
        for s in range(slots):
            swap(0, face, s, mine).start()

    for load in loads[1:]:
        load.wait()

    def index_swap(d, peer_out, slot_in):
        return remote(idx_out.at[peer_out], idx_in.at[slot_in], i_send.at[d], i_recv.at[d],
                      sub_peer(d), grp)

    lane = lax.broadcasted_iota(jnp.int32, (slots, ncs), 1)
    lane_group = jnp.zeros_like(lane)
    for t in range(1, groups):
        lane_group = lane_group + (lane >= per * t).astype(jnp.int32)
    owner_lane = jnp.zeros_like(lane)
    slot_row = lax.broadcasted_iota(jnp.int32, (slots, ncs), 0)
    for g in range(groups):
        for s in range(slots):
            owner_lane = jnp.where((lane_group == g) & (slot_row == s), owners[g, s], owner_lane)
    idx_out[...] = jnp.full(idx_out.shape, -1, jnp.int32)

    def index_for(o):
        idx_out[o, :, 0:ncs] = jnp.where(owner_lane == o, lists[...], -1)

    each(0, n_sub, index_for)
    each(1, n_sub, lambda d: index_swap(d, sub_peer(d), sub).start())
    idx_in[sub] = idx_out[sub]

    shape = (n_sub * per, ncs)
    row = lax.broadcasted_iota(jnp.int32, shape, 0)
    col = lax.broadcasted_iota(jnp.int32, shape, 1)
    col_group = jnp.zeros_like(col)
    for t in range(1, groups):
        col_group = col_group + (col >= per * t).astype(jnp.int32)
    row_tile = jnp.zeros_like(row)
    if n_sub <= 16:
        for t in range(1, n_sub):
            row_tile = row_tile + (row >= per * t).astype(jnp.int32)
    else:
        row_tile = lax.fori_loop(
            1, n_sub, lambda t, a: a + (row >= per * t).astype(jnp.int32), row_tile)
    same = (row - per * row_tile) == (col - per * col_group)
    for s in range(slots):
        named = jnp.full(shape, owners[0, s], jnp.int32)
        for g in range(1, groups):
            named = jnp.where(col_group == g, owners[g, s], named)
        select = jnp.where(same & (named == row_tile), 1.0, 0.0).astype(jnp.bfloat16)
        ordered = dot(select, cmap[s])
        spread[s] = ordered.astype(jnp.bfloat16)
        spread_t[s] = ordered.T

    each(1, n_sub, lambda d: index_swap(d, sub_peer(d), sub_source(d)).wait())
    index = idx_in[...].reshape(n_sub * slots, idx_in.shape[-1])
    place = lax.broadcasted_iota(jnp.int32, (n_sub * slots, tile_rows), 1)
    for j in range(per):
        hit = jnp.zeros((n_sub * slots, tile_rows), F32)
        for g in range(groups):
            c = per * g + j
            hit = hit + jnp.where(index[:, c:c + 1] == place, 1.0, 0.0)
        pick[:, j] = hit.reshape(n_sub, slots, tile_rows)

    arbuf[...] = jnp.zeros_like(arbuf)
    qbuf[...] = jnp.zeros_like(qbuf)
    row_in = lax.broadcasted_iota(jnp.int32, (half, columns), 0)

    def jump(turn, face, s, source):
        other = theirs[turn][face][pslots[face, s]]
        return jnp.where(row_in < fsizes[face, s], source[face, s] - other, 0.0)

    def corners_out(turn, s):
        cbuf[turn, :, s, :] = dot(spread[s], fbuf[s])

    def c_copy(turn, d, slot_in):
        return remote(cbuf.at[turn, pl.ds(sub_peer(d) * per, per)], cin.at[turn, slot_in],
                      c_send.at[turn, d], c_recv.at[turn, d], sub_peer(d), grp)

    def t_copy(turn, d, slot_in):
        return remote(tile.at[turn, grp_peer(d)], tile_in.at[turn, slot_in],
                      t_send.at[turn, d], t_recv.at[turn, d], sub, grp_peer(d))

    def coarse_solve(turn, meanwhile):
        each(1, n_sub, lambda d: c_copy(turn, d, sub).start())
        cin[turn, sub] = cbuf[turn, pl.ds(sub * per, per)]
        local = meanwhile()
        each(1, n_sub, lambda d: c_copy(turn, d, sub_source(d)).wait())
        terms = cin[turn].reshape(n_sub * per * slots, columns)
        hits = pick[...].reshape(n_sub * per * slots, tile_rows)
        part = dot(terms, hits, TN, HIGHEST)
        tile[turn] = part.reshape(n_grp, columns // n_grp, tile_rows)
        each(1, n_grp, lambda d: t_copy(turn, d, grp).start())
        tile_in[turn, grp] = tile[turn, grp]
        each(1, n_grp, lambda d: t_copy(turn, d, grp_source(d)).wait())
        total = jnp.sum(tile_in[turn], axis=0)
        return total, dot(total, coarse[0], NT, HIGHEST), local

    def all_sum(turn):
        def g_copy(d, slot_in):
            return remote(arbuf.at[turn], ar_grp.at[turn, slot_in],
                          g_send.at[turn, d], g_recv.at[turn, d], sub, grp_peer(d))

        def s_copy(d, slot_in):
            return remote(arbuf.at[turn + 2], ar_sub.at[turn, slot_in],
                          s_send.at[turn, d], s_recv.at[turn, d], sub_peer(d), grp)

        each(1, n_grp, lambda d: g_copy(d, grp).start())
        ar_grp[turn, grp] = arbuf[turn]
        each(1, n_grp, lambda d: g_copy(d, grp_source(d)).wait())
        arbuf[turn + 2] = jnp.sum(ar_grp[turn], axis=0)
        each(1, n_sub, lambda d: s_copy(d, sub).start())
        ar_sub[turn, sub] = arbuf[turn + 2]
        each(1, n_sub, lambda d: s_copy(d, sub_source(d)).wait())
        return jnp.sum(ar_sub[turn], axis=0)

    def wait_swap(turn, face, source):
        for s in range(slots):
            swap(turn, face, s, source).wait()

    def store(which, source, target, face):
        return pltpu.make_async_copy(
            source.at[face], target.at[:, pl.ds(face * half, half)], o_sem.at[which, face])

    squares = jnp.zeros((8, columns), F32)
    for face in (0, 1):
        wait_swap(0, face, mine)
        for s in range(slots):
            value = jump(0, face, s, mine)
            resid[face, s] = value
            fbuf[s, face * half:(face + 1) * half] = (value + value).astype(jnp.bfloat16)
            squares = squares + fold(value * value)
            if face:
                corners_out(0, s)

    def solve_first():
        for s in range(slots):
            ybuf[s] = dot(inverse[s], fbuf[s])
        for face in (0, 1):
            store(0, resid, resid_out, face).start()

    total, solved, _ = coarse_solve(0, solve_first)

    def z_copy(d, slot_in):
        return remote(zfull.at[grp], zfull.at[slot_in], z_send.at[d], z_recv.at[d], sub, grp_peer(d))

    zfull[grp] = solved
    each(1, n_grp, lambda d: z_copy(d, grp).start())
    each(1, n_grp, lambda d: z_copy(d, grp_source(d)).wait())
    hits = pick[...].reshape(n_sub * per * slots, tile_rows)
    back = dot(hits, zfull[...].reshape(columns, tile_rows), NT, HIGHEST)
    rbuf[...] = back.reshape(n_sub, per, slots, columns)

    def r_copy(d, slot_in):
        return remote(rbuf.at[sub_peer(d)], rin.at[pl.ds(slot_in * per, per)],
                      r_send.at[d], r_recv.at[d], sub_peer(d), grp)

    each(1, n_sub, lambda d: r_copy(d, sub).start())
    rin[pl.ds(sub * per, per)] = rbuf[sub]
    each(1, n_sub, lambda d: r_copy(d, sub_source(d)).wait())

    products = jnp.zeros((8, columns), F32)
    for s in range(slots):
        lifted = ybuf[s] + dot(spread_t[s], rin[:, s, :], NN, HIGHEST)
        field[1, s] = lifted[half:]
        swap(1, 1, s, field).start()
        field[0, s] = lifted[:half]
        swap(1, 0, s, field).start()
        products = products + fold(lifted[:half] * resid[0, s]) + fold(lifted[half:] * resid[1, s])
    arbuf[0, 0:1] = jnp.sum(squares, axis=0, keepdims=True)
    arbuf[0, 1:2] = 2.0 * jnp.sum(products, axis=0, keepdims=True)
    sums = all_sum(0)
    first = sums[0:1]
    energy = sums[1:2]
    alpha = first / energy

    squares = jnp.zeros((8, columns), F32)
    cross = jnp.zeros((8, columns), F32)
    for face in (0, 1):
        wait_swap(1, face, field)
        for s in range(slots):
            value = jump(1, face, s, field)
            later = resid[face, s] - alpha * value
            image[face, s] = later
            fbuf[s, face * half:(face + 1) * half] = (later + later).astype(jnp.bfloat16)
            squares = squares + fold(later * later)
            cross = cross + fold(later * value)
            if face:
                corners_out(1, s)

    def solve_later():
        for face in (0, 1):
            store(1, image, later_out, face).start()
        sums = jnp.zeros((8, columns), F32)
        for s in range(slots):
            local = dot(inverse[s], fbuf[s])
            sums = sums + fold(local[:half] * image[0, s]) + fold(local[half:] * image[1, s])
        return sums

    total, solved, products = coarse_solve(1, solve_later)
    qbuf[grp] = total * solved
    ones = jnp.ones((8, tile_rows), F32)
    coarse_row = dot(ones, qbuf[...].reshape(columns, tile_rows), NT, HIGHEST)[0:1]
    arbuf[1, 0:1] = jnp.sum(squares, axis=0, keepdims=True)
    arbuf[1, 1:2] = jnp.sum(cross, axis=0, keepdims=True)
    arbuf[1, 2:3] = 2.0 * jnp.sum(products, axis=0, keepdims=True) + coarse_row
    sums = all_sum(1)
    new = sums[0:1]
    beta = new / first
    alpha_later = new / (sums[2:3] + 2.0 * beta * sums[1:2] + beta * beta * energy)
    weight_out[...] = alpha + alpha_later * beta
    alpha_out[...] = alpha_later
    for face in (0, 1):
        store(0, resid, resid_out, face).wait()
        store(1, image, later_out, face).wait()


def body(n_sub, n_grp, gap, inverse, cmap, coarse, pslots, fsizes, owners, lists):
    slots, width, columns = gap.shape
    half = width // 2
    ncs = cmap.shape[1]
    groups = owners.shape[1]
    per = ncs // groups
    tile_rows = coarse.shape[1]
    part = columns // n_grp
    vmem = pl.BlockSpec(memory_space=pltpu.VMEM)
    hbm = pl.BlockSpec(memory_space=pl.ANY)
    faces = pltpu.VMEM((2, slots, half, columns), F32)
    dma = pltpu.SemaphoreType.DMA
    smem = pltpu.SMEM
    scratch = [
        pltpu.VMEM(gap.shape, gap.dtype), pltpu.VMEM(inverse.shape, inverse.dtype),
        pltpu.VMEM(cmap.shape, cmap.dtype), pltpu.VMEM(coarse.shape, coarse.dtype),
        smem((2, slots), jnp.int32), smem((2, slots), jnp.int32), smem((groups, slots), jnp.int32),
        pltpu.VMEM(lists.shape, lists.dtype), dma((8,)), dma((2, 2)),
        faces, faces, *[pltpu.VMEM((slots, half, columns), F32)] * 4, faces,
        pltpu.VMEM((slots, width, columns), jnp.bfloat16),
        pltpu.VMEM((slots, width, columns), F32), faces,
        pltpu.VMEM((slots, n_sub * per, width), jnp.bfloat16),
        pltpu.VMEM((slots, width, n_sub * per), F32),
        pltpu.VMEM((n_sub, slots, 128), jnp.int32),
        pltpu.VMEM((n_sub, slots, 128), jnp.int32),
        pltpu.VMEM((n_sub, per, slots, tile_rows), F32),
        pltpu.VMEM((2, n_sub * per, slots, columns), F32),
        pltpu.VMEM((2, n_sub, per, slots, columns), F32),
        pltpu.VMEM((2, n_grp, part, tile_rows), F32),
        pltpu.VMEM((2, n_grp, part, tile_rows), F32),
        pltpu.VMEM((n_grp, part, tile_rows), F32),
        pltpu.VMEM((n_grp, part, tile_rows), F32),
        pltpu.VMEM((n_sub, per, slots, columns), F32),
        pltpu.VMEM((n_sub * per, slots, columns), F32),
        pltpu.VMEM((4, 8, columns), F32),
        pltpu.VMEM((2, n_grp, 8, columns), F32),
        pltpu.VMEM((2, n_sub, 8, columns), F32),
        dma((2, 2, slots)), dma((2, 2, slots)),
        dma((n_sub,)), dma((n_sub,)),
        dma((2, n_sub)), dma((2, n_sub)),
        dma((2, n_grp)), dma((2, n_grp)),
        dma((n_grp,)), dma((n_grp,)),
        dma((n_sub,)), dma((n_sub,)),
        dma((2, n_grp)), dma((2, n_grp)),
        dma((2, n_sub)), dma((2, n_sub)),
    ]
    whole = jax.ShapeDtypeStruct((slots, width, columns), F32)
    row = jax.ShapeDtypeStruct((1, columns), F32)
    resid, later, weight, alpha = pl.pallas_call(
        functools.partial(kernel, n_sub, n_grp, (slots, half, columns, per, groups, tile_rows)),
        out_shape=(whole, whole, row, row),
        in_specs=[pl.BlockSpec(memory_space=pltpu.HBM)] * 8,
        out_specs=(hbm, hbm, vmem, vmem),
        scratch_shapes=scratch,
        compiler_params=pltpu.CompilerParams(
            collective_id=0, has_side_effects=True, vmem_limit_bytes=VMEM_BYTES),
    )(gap, inverse, cmap, coarse, pslots.T, fsizes.T, owners.T, lists)
    return weight * resid + alpha * later


def solution(mesh):
    wide = P(("sub", "grp"), None, None)
    flat = P(("sub", "grp"), None)
    placed = (wide, wide, wide, P("sub", None, None), flat, flat, flat, flat)
    return jax.shard_map(
        functools.partial(body, mesh.shape["sub"], mesh.shape["grp"]),
        mesh=mesh, in_specs=placed, out_specs=wide, check_vma=False,
    )
```

```python
import functools

import jax
import jax.numpy as jnp
from jax import lax
from jax.experimental import pallas as pl
from jax.experimental.pallas import tpu as pltpu
from jax.sharding import PartitionSpec as P

MESH = pl.DeviceIdType.MESH
VMEM_BYTES = 56 * 1024 * 1024
HIGHEST = lax.Precision.HIGHEST
F32 = jnp.float32
NN = (((1,), (0,)), ((), ()))
NT = (((1,), (1,)), ((), ()))
TN = (((0,), (0,)), ((), ()))


def dot(a, b, dims=NN, precision=None):
    return lax.dot_general(a, b, dims, precision=precision, preferred_element_type=F32)


def thirds(x):
    high = x.astype(jnp.bfloat16)
    rest = x - high.astype(F32)
    middle = rest.astype(jnp.bfloat16)
    return high, middle, (rest - middle.astype(F32)).astype(jnp.bfloat16)


def each(low, high, step):
    if high - low <= 16:
        for i in range(low, high):
            step(i)
    else:
        lax.fori_loop(low, high, lambda i, c: (step(i), c)[1], 0)


def fold(x):
    rows, columns = x.shape
    return jnp.sum(x.reshape(rows // 8, 8, columns), axis=0)


def kernel(
    n_sub, n_grp, dims,
    gap_in, inverse_in, cmap_in, coarse_in, pslots_in, fsizes_in, owners_in, lists_in,
    resid_out, later_out, weight_out, alpha_out,
    gap, inverse, cmap, coarse, pslots, fsizes, owners, lists, l_sem, o_sem,
    mine, field, near_first, far_first, near_later, far_later, resid, fbuf, ybuf, image,
    spread, spread_t, idx_out, idx_in, pick, cbuf, cin, tile, tile_in, zfull, qbuf, rbuf, rin,
    arbuf, ar_grp, ar_sub,
    x_send, x_recv, i_send, i_recv, c_send, c_recv, t_send, t_recv, z_send, z_recv, r_send, r_recv,
    g_send, g_recv, s_send, s_recv,
):
    slots, half, columns, per, groups, tile_rows = dims
    ncs = per * groups
    sub = lax.axis_index("sub")
    grp = lax.axis_index("grp")
    top = n_sub // 2
    theirs = ((near_first, far_first), (near_later, far_later))

    def flip(bit):
        return sub + bit - 2 * bit * (sub // bit % 2)

    def sub_peer(d):
        return lax.rem(sub + d, n_sub)

    def sub_source(d):
        return lax.rem(sub + n_sub - d, n_sub)

    def grp_peer(d):
        return lax.rem(grp + d, n_grp)

    def grp_source(d):
        return lax.rem(grp + n_grp - d, n_grp)

    def remote(src, dst, send, recv, to_sub, to_grp):
        return pltpu.make_async_remote_copy(
            src_ref=src, dst_ref=dst, send_sem=send, recv_sem=recv,
            device_id=(to_sub, to_grp), device_id_type=MESH,
        )

    loads = [
        pltpu.make_async_copy(source, target, l_sem.at[i])
        for i, (source, target) in enumerate((
            (gap_in, gap), (lists_in, lists), (owners_in, owners), (cmap_in, cmap),
            (inverse_in, inverse), (coarse_in, coarse), (pslots_in, pslots), (fsizes_in, fsizes)))
    ]
    for load in loads:
        load.start()
    barrier = pltpu.get_barrier_semaphore()
    each(1, n_sub, lambda d: pl.semaphore_signal(
        barrier, inc=1, device_id=(sub_peer(d), grp), device_id_type=MESH))
    each(1, n_grp, lambda d: pl.semaphore_signal(
        barrier, inc=1, device_id=(sub, grp_peer(d)), device_id_type=MESH))

    loads[0].wait()
    for s in range(slots):
        wide = gap[s].astype(F32)
        mine[0, s] = wide[:half]
        mine[1, s] = wide[half:]
    pl.semaphore_wait(barrier, n_sub + n_grp - 2)

    def swap(turn, face, s, source):
        return remote(
            source.at[face, s], theirs[turn][face].at[s], x_send.at[turn, face, s],
            x_recv.at[turn, face, s], flip(top) if face else flip(1), grp)

    for face in (1, 0):
        for s in range(slots):
            swap(0, face, s, mine).start()

    for load in loads[1:]:
        load.wait()

    def index_swap(d, peer_out, slot_in):
        return remote(idx_out.at[peer_out], idx_in.at[slot_in], i_send.at[d], i_recv.at[d],
                      sub_peer(d), grp)

    lane = lax.broadcasted_iota(jnp.int32, (slots, ncs), 1)
    lane_group = jnp.zeros_like(lane)
    for t in range(1, groups):
        lane_group = lane_group + (lane >= per * t).astype(jnp.int32)
    owner_lane = jnp.zeros_like(lane)
    slot_row = lax.broadcasted_iota(jnp.int32, (slots, ncs), 0)
    for g in range(groups):
        for s in range(slots):
            owner_lane = jnp.where((lane_group == g) & (slot_row == s), owners[g, s], owner_lane)
    idx_out[...] = jnp.full(idx_out.shape, -1, jnp.int32)

    def index_for(o):
        idx_out[o, :, 0:ncs] = jnp.where(owner_lane == o, lists[...], -1)

    each(0, n_sub, index_for)
    each(1, n_sub, lambda d: index_swap(d, sub_peer(d), sub).start())
    idx_in[sub] = idx_out[sub]

    shape = (n_sub * per, ncs)
    row = lax.broadcasted_iota(jnp.int32, shape, 0)
    col = lax.broadcasted_iota(jnp.int32, shape, 1)
    col_group = jnp.zeros_like(col)
    for t in range(1, groups):
        col_group = col_group + (col >= per * t).astype(jnp.int32)
    row_tile = jnp.zeros_like(row)
    if n_sub <= 16:
        for t in range(1, n_sub):
            row_tile = row_tile + (row >= per * t).astype(jnp.int32)
    else:
        row_tile = lax.fori_loop(
            1, n_sub, lambda t, a: a + (row >= per * t).astype(jnp.int32), row_tile)
    same = (row - per * row_tile) == (col - per * col_group)
    for s in range(slots):
        named = jnp.full(shape, owners[0, s], jnp.int32)
        for g in range(1, groups):
            named = jnp.where(col_group == g, owners[g, s], named)
        select = jnp.where(same & (named == row_tile), 1.0, 0.0).astype(jnp.bfloat16)
        ordered = dot(select, cmap[s])
        spread[s] = ordered.astype(jnp.bfloat16)
        spread_t[s] = ordered.T

    each(1, n_sub, lambda d: index_swap(d, sub_peer(d), sub_source(d)).wait())
    index = idx_in[...].reshape(n_sub * slots, idx_in.shape[-1])
    place = lax.broadcasted_iota(jnp.int32, (n_sub * slots, tile_rows), 1)
    for j in range(per):
        hit = jnp.zeros((n_sub * slots, tile_rows), F32)
        for g in range(groups):
            c = per * g + j
            hit = hit + jnp.where(index[:, c:c + 1] == place, 1.0, 0.0)
        pick[:, j] = hit.reshape(n_sub, slots, tile_rows)

    arbuf[...] = jnp.zeros_like(arbuf)
    qbuf[...] = jnp.zeros_like(qbuf)
    row_in = lax.broadcasted_iota(jnp.int32, (half, columns), 0)

    def jump(turn, face, s, source):
        other = theirs[turn][face][pslots[face, s]]
        return jnp.where(row_in < fsizes[face, s], source[face, s] - other, 0.0)

    def corners_out(turn, s):
        cbuf[turn, :, s, :] = dot(spread[s], fbuf[s])

    def c_copy(turn, d, slot_in):
        return remote(cbuf.at[turn, pl.ds(sub_peer(d) * per, per)], cin.at[turn, slot_in],
                      c_send.at[turn, d], c_recv.at[turn, d], sub_peer(d), grp)

    def t_copy(turn, d, slot_in):
        return remote(tile.at[turn, grp_peer(d)], tile_in.at[turn, slot_in],
                      t_send.at[turn, d], t_recv.at[turn, d], sub, grp_peer(d))

    def coarse_solve(turn, meanwhile):
        each(1, n_sub, lambda d: c_copy(turn, d, sub).start())
        cin[turn, sub] = cbuf[turn, pl.ds(sub * per, per)]
        local = meanwhile()
        each(1, n_sub, lambda d: c_copy(turn, d, sub_source(d)).wait())
        terms = cin[turn].reshape(n_sub * per * slots, columns)
        hits = pick[...].reshape(n_sub * per * slots, tile_rows)
        hits = hits.astype(jnp.bfloat16)
        part = sum(dot(third, hits, TN) for third in thirds(terms))
        tile[turn] = part.reshape(n_grp, columns // n_grp, tile_rows)
        each(1, n_grp, lambda d: t_copy(turn, d, grp).start())
        tile_in[turn, grp] = tile[turn, grp]
        each(1, n_grp, lambda d: t_copy(turn, d, grp_source(d)).wait())
        total = jnp.sum(tile_in[turn], axis=0)
        return total, dot(total, coarse[0], NT, HIGHEST), local

    def all_sum(turn):
        def g_copy(d, slot_in):
            return remote(arbuf.at[turn], ar_grp.at[turn, slot_in],
                          g_send.at[turn, d], g_recv.at[turn, d], sub, grp_peer(d))

        def s_copy(d, slot_in):
            return remote(arbuf.at[turn + 2], ar_sub.at[turn, slot_in],
                          s_send.at[turn, d], s_recv.at[turn, d], sub_peer(d), grp)

        each(1, n_grp, lambda d: g_copy(d, grp).start())
        ar_grp[turn, grp] = arbuf[turn]
        each(1, n_grp, lambda d: g_copy(d, grp_source(d)).wait())
        arbuf[turn + 2] = jnp.sum(ar_grp[turn], axis=0)
        each(1, n_sub, lambda d: s_copy(d, sub).start())
        ar_sub[turn, sub] = arbuf[turn + 2]
        each(1, n_sub, lambda d: s_copy(d, sub_source(d)).wait())
        return jnp.sum(ar_sub[turn], axis=0)

    def wait_swap(turn, face, source):
        for s in range(slots):
            swap(turn, face, s, source).wait()

    def store(which, source, target, face):
        return pltpu.make_async_copy(
            source.at[face], target.at[:, pl.ds(face * half, half)], o_sem.at[which, face])

    squares = jnp.zeros((8, columns), F32)
    for face in (0, 1):
        wait_swap(0, face, mine)
        for s in range(slots):
            value = jump(0, face, s, mine)
            resid[face, s] = value
            fbuf[s, face * half:(face + 1) * half] = (value + value).astype(jnp.bfloat16)
            squares = squares + fold(value * value)
            if face:
                corners_out(0, s)

    def solve_first():
        for s in range(slots):
            ybuf[s] = dot(inverse[s], fbuf[s])
        for face in (0, 1):
            store(0, resid, resid_out, face).start()

    total, solved, _ = coarse_solve(0, solve_first)

    def z_copy(d, slot_in):
        return remote(zfull.at[grp], zfull.at[slot_in], z_send.at[d], z_recv.at[d], sub, grp_peer(d))

    zfull[grp] = solved
    each(1, n_grp, lambda d: z_copy(d, grp).start())
    each(1, n_grp, lambda d: z_copy(d, grp_source(d)).wait())
    hits = pick[...].reshape(n_sub * per * slots, tile_rows)
    hits = hits.astype(jnp.bfloat16)
    back = sum(dot(hits, third, NT) for third in thirds(zfull[...].reshape(columns, tile_rows)))
    rbuf[...] = back.reshape(n_sub, per, slots, columns)

    def r_copy(d, slot_in):
        return remote(rbuf.at[sub_peer(d)], rin.at[pl.ds(slot_in * per, per)],
                      r_send.at[d], r_recv.at[d], sub_peer(d), grp)

    each(1, n_sub, lambda d: r_copy(d, sub).start())
    rin[pl.ds(sub * per, per)] = rbuf[sub]
    each(1, n_sub, lambda d: r_copy(d, sub_source(d)).wait())

    products = jnp.zeros((8, columns), F32)
    for s in range(slots):
        lifted = ybuf[s] + dot(spread_t[s], rin[:, s, :], NN, HIGHEST)
        field[1, s] = lifted[half:]
        swap(1, 1, s, field).start()
        field[0, s] = lifted[:half]
        swap(1, 0, s, field).start()
        products = products + fold(lifted[:half] * resid[0, s]) + fold(lifted[half:] * resid[1, s])
    arbuf[0, 0:1] = jnp.sum(squares, axis=0, keepdims=True)
    arbuf[0, 1:2] = 2.0 * jnp.sum(products, axis=0, keepdims=True)
    sums = all_sum(0)
    first = sums[0:1]
    energy = sums[1:2]
    alpha = first / energy

    squares = jnp.zeros((8, columns), F32)
    cross = jnp.zeros((8, columns), F32)
    for face in (0, 1):
        wait_swap(1, face, field)
        for s in range(slots):
            value = jump(1, face, s, field)
            later = resid[face, s] - alpha * value
            image[face, s] = later
            fbuf[s, face * half:(face + 1) * half] = (later + later).astype(jnp.bfloat16)
            squares = squares + fold(later * later)
            cross = cross + fold(later * value)
            if face:
                corners_out(1, s)

    def solve_later():
        for face in (0, 1):
            store(1, image, later_out, face).start()
        sums = jnp.zeros((8, columns), F32)
        for s in range(slots):
            local = dot(inverse[s], fbuf[s])
            sums = sums + fold(local[:half] * image[0, s]) + fold(local[half:] * image[1, s])
        return sums

    total, solved, products = coarse_solve(1, solve_later)
    qbuf[grp] = total * solved
    ones = jnp.ones((8, tile_rows), F32)
    coarse_row = dot(ones, qbuf[...].reshape(columns, tile_rows), NT, HIGHEST)[0:1]
    arbuf[1, 0:1] = jnp.sum(squares, axis=0, keepdims=True)
    arbuf[1, 1:2] = jnp.sum(cross, axis=0, keepdims=True)
    arbuf[1, 2:3] = 2.0 * jnp.sum(products, axis=0, keepdims=True) + coarse_row
    sums = all_sum(1)
    new = sums[0:1]
    beta = new / first
    alpha_later = new / (sums[2:3] + 2.0 * beta * sums[1:2] + beta * beta * energy)
    weight_out[...] = alpha + alpha_later * beta
    alpha_out[...] = alpha_later
    for face in (0, 1):
        store(0, resid, resid_out, face).wait()
        store(1, image, later_out, face).wait()


def body(n_sub, n_grp, gap, inverse, cmap, coarse, pslots, fsizes, owners, lists):
    slots, width, columns = gap.shape
    half = width // 2
    ncs = cmap.shape[1]
    groups = owners.shape[1]
    per = ncs // groups
    tile_rows = coarse.shape[1]
    part = columns // n_grp
    vmem = pl.BlockSpec(memory_space=pltpu.VMEM)
    hbm = pl.BlockSpec(memory_space=pl.ANY)
    faces = pltpu.VMEM((2, slots, half, columns), F32)
    dma = pltpu.SemaphoreType.DMA
    smem = pltpu.SMEM
    scratch = [
        pltpu.VMEM(gap.shape, gap.dtype), pltpu.VMEM(inverse.shape, inverse.dtype),
        pltpu.VMEM(cmap.shape, cmap.dtype), pltpu.VMEM(coarse.shape, coarse.dtype),
        smem((2, slots), jnp.int32), smem((2, slots), jnp.int32), smem((groups, slots), jnp.int32),
        pltpu.VMEM(lists.shape, lists.dtype), dma((8,)), dma((2, 2)),
        faces, faces, *[pltpu.VMEM((slots, half, columns), F32)] * 4, faces,
        pltpu.VMEM((slots, width, columns), jnp.bfloat16),
        pltpu.VMEM((slots, width, columns), F32), faces,
        pltpu.VMEM((slots, n_sub * per, width), jnp.bfloat16),
        pltpu.VMEM((slots, width, n_sub * per), F32),
        pltpu.VMEM((n_sub, slots, 128), jnp.int32),
        pltpu.VMEM((n_sub, slots, 128), jnp.int32),
        pltpu.VMEM((n_sub, per, slots, tile_rows), F32),
        pltpu.VMEM((2, n_sub * per, slots, columns), F32),
        pltpu.VMEM((2, n_sub, per, slots, columns), F32),
        pltpu.VMEM((2, n_grp, part, tile_rows), F32),
        pltpu.VMEM((2, n_grp, part, tile_rows), F32),
        pltpu.VMEM((n_grp, part, tile_rows), F32),
        pltpu.VMEM((n_grp, part, tile_rows), F32),
        pltpu.VMEM((n_sub, per, slots, columns), F32),
        pltpu.VMEM((n_sub * per, slots, columns), F32),
        pltpu.VMEM((4, 8, columns), F32),
        pltpu.VMEM((2, n_grp, 8, columns), F32),
        pltpu.VMEM((2, n_sub, 8, columns), F32),
        dma((2, 2, slots)), dma((2, 2, slots)),
        dma((n_sub,)), dma((n_sub,)),
        dma((2, n_sub)), dma((2, n_sub)),
        dma((2, n_grp)), dma((2, n_grp)),
        dma((n_grp,)), dma((n_grp,)),
        dma((n_sub,)), dma((n_sub,)),
        dma((2, n_grp)), dma((2, n_grp)),
        dma((2, n_sub)), dma((2, n_sub)),
    ]
    whole = jax.ShapeDtypeStruct((slots, width, columns), F32)
    row = jax.ShapeDtypeStruct((1, columns), F32)
    resid, later, weight, alpha = pl.pallas_call(
        functools.partial(kernel, n_sub, n_grp, (slots, half, columns, per, groups, tile_rows)),
        out_shape=(whole, whole, row, row),
        in_specs=[pl.BlockSpec(memory_space=pltpu.HBM)] * 8,
        out_specs=(hbm, hbm, vmem, vmem),
        scratch_shapes=scratch,
        compiler_params=pltpu.CompilerParams(
            collective_id=0, has_side_effects=True, vmem_limit_bytes=VMEM_BYTES),
    )(gap, inverse, cmap, coarse, pslots.T, fsizes.T, owners.T, lists)
    return weight * resid + alpha * later


def solution(mesh):
    wide = P(("sub", "grp"), None, None)
    flat = P(("sub", "grp"), None)
    placed = (wide, wide, wide, P("sub", None, None), flat, flat, flat, flat)
    return jax.shard_map(
        functools.partial(body, mesh.shape["sub"], mesh.shape["grp"]),
        mesh=mesh, in_specs=placed, out_specs=wide, check_vma=False,
    )
```
